32 devices in a mesh: rows: 8 (over z, x), feat: 4 (over y, core).
Axes of the slice: x: 2, y: 2, z: 4, core: 2. Of those that a mesh axis runs over, the one named last changes fastest.
Arguments:
- slab_rows: bfloat16 [4096, 2048], P('rows', 'feat'), may hold values from -0.125 to 0.125
- labels: int32 [4096], P('rows'), may hold values 0 or 1
- center: float32 [2048], P('feat'), may hold values from -4 to 4
- theta_start: float32 [64, 2048], P(None, 'feat'), may hold values from -4 to 4
- momentum: float32 [64, 2048], P(None, 'feat'), may hold values from -6 to 6
- step_size: float32 [64], replicated, may hold values from 0.5 to 2
- sample_index: int32 [8192], P('rows'), may hold values from 0 to 511
- sample_count: int32 [8], P('rows'), may hold values from 128 to 1024, as said below
Outputs:
- theta_end: float32 [64, 2048], P(None, 'feat')
- momentum_end: float32 [64, 2048], P(None, 'feat')
- hessian: float32 [2048, 2048], P('feat', 'rows')
The draws below stay inside these ranges and needn't reach their ends.
Inputs may be any that keep to these rules, and one draw needn't show every extreme that they name: `sample_index`: row numbers in slots that are not live are arbitrary and unused. `sample_count`: A multiple of 128; some index of rows holds exactly 1024 live slots.
All inputs are finite; a program needn't handle non-finite values. No bound on the sum of `labels` on one device may be relied on, other than what follows from the above.
Results may differ from the reference program's by a relative error of at most 0.0063.
Values may be sent and summed in bfloat16 or wider, within the bound.
A program may use at most 64 MiB of HBM per device.

```python
import math
import jax
import jax.numpy as jnp
from jax import lax

D = 2048
CHAINS = 64
STEPS = 2
SUB_BLOCK = 128
SUB_BLOCKS = 8
SLAB_DEV = 512
SLAB = 4096
CAPACITY = 1024
SAMPLES = 8192
N_ROWS = 8


def draw_sample_count(key, part):
    blocks = jax.random.randint(key, (N_ROWS,), 1, 5)
    busiest = jax.random.randint(jax.random.fold_in(key, 7), (), 0, N_ROWS)
    blocks = jnp.where(jnp.arange(N_ROWS) == busiest, SUB_BLOCKS, blocks)
    return (blocks * SUB_BLOCK).astype(jnp.int32)


def set_ends(values, stream_key, least, largest):
    extent = values.shape
    index_at = [jax.random.randint(jax.random.fold_in(stream_key, axis), (), 0, extent[axis]) for axis in range(len(extent))]
    values = values.at[tuple(index_at)].set(least)
    longest = extent.index(max(extent))
    index_at[longest] = (index_at[longest] + 1) % extent[longest]
    return values.at[tuple(index_at)].set(largest)


def steps_of(rng, extent, pieces, low, largest):
    gain = 1.0
    for dim, parts in pieces:
        steps = jax.random.uniform(jax.random.fold_in(jax.random.fold_in(rng, 6), dim), (parts,), jnp.float32, low / len(pieces), largest / len(pieces))
        gain = gain * jnp.repeat(jnp.exp(steps), extent[dim] // parts).reshape((-1,) + (1,) * (len(extent) - 1 - dim))
    return gain


def centred(stream_key, dims, deviation, most, pieces=(), kind=jnp.bfloat16):
    entries = jax.random.normal(stream_key, dims, jnp.float32) * deviation
    if len(pieces) > 0:
        entries = steps_of(stream_key, dims, pieces, -0.22, 0.18) * entries
    return jnp.clip(entries, min=-most, max=most).astype(kind)


def setup_inputs(seed: int = 0) -> dict:
    streams_of = jax.random.split(jax.random.key(seed), 9)
    return {
        "slab_rows": centred(streams_of[0], (SLAB, D), D ** -0.5, 0.125, ((0, 8), (1, 4))),
        "labels": set_ends((jax.random.randint(streams_of[1], (SLAB,), 0, 2) < 1).astype(jnp.int32), jax.random.fold_in(streams_of[1], 1), 0, 1),
        "center": centred(streams_of[2], (D,), 0.7, 4.0, ((0, 4),), jnp.float32),
        "theta_start": centred(streams_of[3], (CHAINS, D), 0.7, 4.0, ((1, 4),), jnp.float32),
        "momentum": centred(streams_of[4], (CHAINS, D), 1.0, 6.0, ((1, 4),), jnp.float32),
        "step_size": jnp.clip(jnp.exp(jax.random.uniform(streams_of[5], (CHAINS,), jnp.float32, math.log(0.5), math.log(2.0))), 0.5, 2.0),
        "sample_index": set_ends(jax.random.randint(streams_of[6], (SAMPLES,), 0, SLAB_DEV), jax.random.fold_in(streams_of[6], 1), 0, SLAB_DEV - 1).astype(jnp.int32),
        "sample_count": draw_sample_count(jax.random.fold_in(streams_of[8], 71), 0),
    }


def reference(slab_rows, labels, center, theta_start, momentum, step_size, sample_index, sample_count):
    center_bf = center.astype(jnp.bfloat16)
    logit_hat = jnp.dot(slab_rows, center_bf, preferred_element_type=jnp.float32)
    prob_hat = jax.nn.sigmoid(logit_hat)
    weight = prob_hat * (1.0 - prob_hat)
    residual = labels.astype(jnp.float32) - prob_hat

    def accumulate(total_sum, number):
        first_row = (number * SLAB_DEV).astype(jnp.int32)
        rows_here = lax.dynamic_slice_in_dim(slab_rows, first_row, SLAB_DEV, 0)
        weight_here = lax.dynamic_slice_in_dim(weight, first_row, SLAB_DEV, 0)
        scaled = (weight_here[:, None] * rows_here).astype(jnp.bfloat16)
        product = lax.dot_general(scaled, rows_here, (((0,), (0,)), ((), ())), preferred_element_type=jnp.float32)
        return (total_sum + product, None)
    hessian, _ = lax.scan(accumulate, jnp.zeros((D, D), jnp.float32), jnp.arange(N_ROWS, dtype=jnp.int32))
    grad_hat = jnp.dot(residual.astype(jnp.bfloat16), slab_rows, preferred_element_type=jnp.float32)
    sample_total = jnp.sum(sample_count).astype(jnp.float32)
    slots = jnp.arange(N_ROWS * CAPACITY, dtype=jnp.int32)
    device_of = slots // CAPACITY
    global_rows = device_of * SLAB_DEV + sample_index.astype(jnp.int32)
    live_mask = slots % CAPACITY < sample_count[device_of]
    picked = jnp.take(slab_rows, global_rows, axis=0)
    logit_ref = jnp.take(logit_hat, global_rows)[:, None]
    weight_ref = jnp.take(weight, global_rows)[:, None]
    prob_ref = jax.nn.sigmoid(logit_ref)
    leap_size = step_size[:, None] * math.sqrt(D / SLAB)

    def gradient(position):
        offset = position - center[None, :]
        curvature = jnp.dot(offset, hessian.T, precision=lax.Precision.HIGHEST)
        logit_now = jnp.dot(picked, position.astype(jnp.bfloat16).T, preferred_element_type=jnp.float32)
        remainder = prob_ref - jax.nn.sigmoid(logit_now) + weight_ref * (logit_now - logit_ref)
        remainder = jnp.where(live_mask[:, None], remainder, 0.0).astype(jnp.bfloat16)
        correction = jnp.dot(remainder.T, picked, preferred_element_type=jnp.float32)
        return grad_hat[None, :] - curvature + SLAB / sample_total * correction - position
    position = theta_start
    moment = momentum + 0.5 * leap_size * gradient(position)
    for leap_index in range(STEPS):
        position = position + leap_size * moment
        factor = leap_size if leap_index + 1 < STEPS else 0.5 * leap_size
        moment = moment + factor * gradient(position)
    return (position, moment, hessian)
```

```python
import functools
import math

import jax
import jax.numpy as jnp
from jax import lax
from jax.experimental import pallas as pl
from jax.experimental.pallas import tpu as pltpu
from jax.sharding import PartitionSpec as P

STEPS = 2
LANES = 128
PIECES = 4
MESH = pl.DeviceIdType.MESH
F32, BF16 = jnp.float32, jnp.bfloat16


def each(count, body, limit=8):
    if count <= limit:
        for number in range(count):
            body(number)
    else:
        lax.fori_loop(0, count, lambda number, none: (body(number), none)[1], 0)


def dot(left, right, left_dim, right_dim):
    return lax.dot_general(
        left, right, (((left_dim,), (right_dim,)), ((), ())), preferred_element_type=F32
    )


def split(value):
    high = value.astype(BF16)
    return high, (value - high.astype(F32)).astype(BF16)


def kernel(
    R, F, S, whole_rows,
    x_ref, label_ref, mult_ref, count_ref, center_ref, theta_ref, mom_ref, leap_ref,
    theta_out, mom_out, hess_out,
    x_full, theta_full, mom_full, center_full, count_full,
    c_send, c_recv, state, state_recv, final_recv,
    h_part, h_send, h_recv, h_send2, h_recv2,
    x_ssem, x_rsem, x_fsem, s_ssem, s_rsem, n_ssem, n_rsem,
    c_ssem, c_rsem, p_ssem, p_rsem, o_ssem, o_rsem,
    h_ssem, h_rsem, g_ssem, g_rsem,
):
    rows, wide = x_ref.shape
    group = theta_ref.shape[0] // F
    w = c_send.shape[-1]
    per = wide // w
    A = R // 2
    cw = hess_out.shape[0]
    r, f = lax.axis_index("rows"), lax.axis_index("feat")
    a, b = r // 2, lax.rem(r, 2)
    mate = f + 1 - 2 * lax.rem(f, 2)
    piece = rows // PIECES

    def copy(src, dst, ssem, rsem, row, feat):
        return pltpu.make_async_remote_copy(
            src_ref=src, dst_ref=dst, send_sem=ssem, recv_sem=rsem,
            device_id=(row, feat), device_id_type=MESH,
        )

    def row_peer(i):
        return lax.rem(r + i + 1, R)

    barrier = pltpu.get_barrier_semaphore()

    def greet_row(i):
        pl.semaphore_signal(barrier, inc=1, device_id=(row_peer(i), f), device_id_type=MESH)

    def greet_feat(i):
        pl.semaphore_signal(
            barrier, inc=1, device_id=(r, lax.rem(f + i + 1, F)), device_id_type=MESH
        )

    each(R - 1, greet_row)
    each(F - 1, greet_feat)
    pl.semaphore_wait(barrier, R + F - 2)

    def small(i, number):
        peer = lax.rem(f + i + 1, F)
        theirs = pl.ds(pl.multiple_of(peer * group, group), group)
        src = (center_ref, theta_ref.at[theirs], mom_ref.at[theirs])[number]
        dst = (center_full, theta_full, mom_full)[number].at[f]
        return copy(src, dst, s_ssem.at[number, peer], s_rsem.at[number, f], r, peer)

    def small_in(i, number):
        peer = lax.rem(f + i + 1, F)
        dst = (center_full, theta_full, mom_full)[number].at[peer]
        return copy(dst, dst, s_ssem.at[number, peer], s_rsem.at[number, peer], r, peer)

    def part(c):
        return pl.ds(c * piece, piece)

    def x_out(i, c):
        peer = mate if i == 0 else lax.rem(f + 2 * i, F)
        return copy(
            x_ref.at[part(c)], x_full.at[f, part(c)], x_ssem.at[i, c], x_rsem.at[f, c], r, peer
        )

    def x_in(block, c):
        dst = x_full.at[block, part(c)]
        return copy(dst, dst, x_ssem.at[0, c], x_rsem.at[block, c], r, mate)

    def x_forward(i, c):
        block = lax.rem(f + 2 * i, F)
        dst = x_full.at[block, part(c)]
        return copy(dst, dst, x_fsem.at[i, c], x_rsem.at[block, c], r, mate)

    def count_out(i):
        peer = row_peer(i)
        return copy(count_ref, count_full.at[r], n_ssem.at[peer], n_rsem.at[r], peer, f)

    def count_in(i):
        peer = row_peer(i)
        dst = count_full.at[peer]
        return copy(dst, dst, n_ssem.at[peer], n_rsem.at[peer], peer, f)

    for c in range(PIECES):
        for i in range(1, F // 2):
            x_out(i, c).start()
        if c == 0:
            for i in range(F - 1):
                for number in range(3):
                    small(i, number).start()
            each(R - 1, lambda i: count_out(i).start())
    for c in range(PIECES):
        x_out(0, c).start()

    mine = pl.ds(pl.multiple_of(f * group, group), group)
    center_full[f] = center_ref[...]
    theta_full[f] = theta_ref[mine]
    mom_full[f] = mom_ref[mine]
    x_full[f] = x_ref[...]
    count_full[r] = count_ref[...]
    leap = leap_ref[mine, :]

    for i in range(F - 1):
        for number in range(3):
            small_in(i, number).wait_recv()
    each(R - 1, lambda i: count_in(i).wait_recv())
    total = lax.fori_loop(0, R, lambda i, acc: acc + count_full[i], jnp.zeros_like(count_ref))
    ratio = float(whole_rows) / total[:1, :1]

    for c in range(PIECES):
        for i in range(1, F // 2):
            x_in(lax.rem(f + 2 * i, F), c).wait_recv()
            x_forward(i, c).start()
    for c in range(PIECES):
        x_in(mate, c).wait_recv()
    for c in range(PIECES):
        for i in range(1, F // 2):
            x_in(lax.rem(mate + 2 * i, F), c).wait_recv()

    at_center = jnp.zeros((2 * group, rows), F32)
    for g in range(F):
        high, low = split(center_full[g])
        at_center += dot(jnp.concatenate([high, low], 0), x_full[g], 1, 1)
    logit_hat = at_center[:1]
    center_all = at_center[:1] + at_center[group : group + 1]
    prob_hat = jax.nn.sigmoid(logit_hat)
    weight = prob_hat * (1.0 - prob_hat)
    residual = (label_ref[...] - prob_hat).astype(BF16).astype(F32)
    mult_ratio = mult_ref[...] * ratio

    def c_out(e, i):
        peer = row_peer(i)
        return copy(
            c_send.at[e, lax.rem(peer, S)], c_recv.at[e, r], c_ssem.at[e, peer],
            c_rsem.at[e, r], peer, f,
        )

    def c_in(e, i):
        peer = row_peer(i)
        dst = c_recv.at[e, peer]
        return copy(dst, dst, c_ssem.at[e, peer], c_rsem.at[e, peer], peer, f)

    def on_owner(number, body):
        if S == R:
            body()
        else:
            pl.when(number < S)(body)

    def contribute(e, chunk_of):
        now = jnp.zeros((2 * group, rows), F32)
        for k in range(S):
            high, low = split(chunk_of(k))
            columns = x_full[k // per, :, (k % per) * w : (k % per + 1) * w]
            now += dot(jnp.concatenate([high, low], 0), columns, 1, 1)
        logit_now = now[:group]
        offset = now[:group] + now[group:] - center_all
        remainder = prob_hat - jax.nn.sigmoid(logit_now) + weight * (logit_now - logit_hat)
        remainder = remainder.astype(BF16).astype(F32)
        coef = residual - weight * offset + mult_ratio * remainder
        high, low = split(coef)
        both = jnp.concatenate([high, low], 0)
        for g in range(F):
            value = dot(both, x_full[g], 1, 0)
            value = value[:group] + value[group:]
            for h in range(per):
                c_send[e, g * per + h] = value[:, h * w : (h + 1) * w]

        def send(i):
            on_owner(row_peer(i), lambda: c_out(e, i).start())

        each(R - 1, send)

    def reduced(e):
        on_owner(r, lambda: each(R - 1, lambda i: c_in(e, i).wait_recv()))
        c_recv[e, r] = c_send[e, lax.rem(r, S)]
        return lax.fori_loop(0, R, lambda i, acc: acc + c_recv[e, i], jnp.zeros((group, w), F32))

    def p_out(e, i):
        peer = row_peer(i)
        own = lax.rem(r, S)
        return copy(
            state.at[e], state_recv.at[e, own], p_ssem.at[e, peer], p_rsem.at[e, own], peer, f
        )

    def p_in(e, i):
        peer = lax.rem(row_peer(i), S)
        dst = state_recv.at[e, peer]
        return copy(dst, dst, p_ssem.at[e, peer], p_rsem.at[e, peer], row_peer(i), f)

    def spread(e):
        each(R - 1, lambda i: p_out(e, i).start())
        state_recv[e, lax.rem(r, S)] = state[e]

    def gathered(e):
        def take(i):
            on_owner(row_peer(i), lambda: p_in(e, i).wait_recv())

        each(R - 1, take)

    def h_out(pair):
        rows_there = pl.ds(pl.multiple_of((2 * pair + 1 - b) * cw, cw), cw)
        return copy(
            h_send.at[rows_there], h_recv.at[pair], h_ssem.at[pair], h_rsem.at[pair],
            2 * a + 1 - b, f,
        )

    def g_out(pair):
        return copy(
            h_send2.at[pair], h_recv2.at[a], g_ssem.at[pair], g_rsem.at[a], 2 * pair + b, f
        )

    def g_in(pair):
        dst = h_recv2.at[pair]
        return copy(dst, dst, g_ssem.at[pair], g_rsem.at[pair], 2 * pair + b, f)

    many = A // F

    def block_at(i):
        return lax.rem(a // many + 1 + i, F)

    def h_start():
        column = jnp.transpose(jnp.broadcast_to(weight, (LANES, rows)))[:, :1]
        scaled = (column * x_ref[...].astype(F32)).astype(BF16)

        for i in range(F):
            g = block_at(i)
            value = dot(x_full[g], scaled, 0, 0)
            where = pl.ds(pl.multiple_of(g * wide, wide), wide)
            h_part[where, :] = value
            h_send[where, :] = value.astype(BF16)
            each(many, lambda j: h_out(g * many + j).start())

    def h_pass(i):
        def one(j):
            pair = block_at(i) * many + j
            h_out(pair).wait_recv()
            own = pl.ds(pl.multiple_of((2 * pair + b) * cw, cw), cw)
            value = h_part[own, :] + h_recv[pair].astype(F32)

            @pl.when(pair == a)
            def _():
                hess_out[...] = value

            @pl.when(pair != a)
            def _():
                h_send2[pair] = value.astype(BF16)
                g_out(pair).start()

        each(many, one)

    def o_out(number, i):
        peer = lax.rem(f + i + 1, F)
        theirs = pl.ds(peer * per, per)
        return copy(
            state_recv.at[STEPS - 1 + number, theirs], final_recv.at[number, f], o_ssem.at[number, peer],
            o_rsem.at[number, f], r, peer,
        )

    def o_in(number, i):
        peer = lax.rem(f + i + 1, F)
        dst = final_recv.at[number, peer]
        return copy(dst, dst, o_ssem.at[number, peer], o_rsem.at[number, peer], r, peer)

    def finish(number):
        for i in range(F - 1):
            o_out(number, i).start()
        for h in range(per):
            final_recv[number, f, h] = state_recv[STEPS - 1 + number, f * per + h]

    def write(number, out):
        for i in range(F - 1):
            o_in(number, i).wait_recv()
        for g in range(F):
            for h in range(per):
                out[g * group : (g + 1) * group, h * w : (h + 1) * w] = final_recv[number, g, h]

    own = lax.rem(r, S)

    def own_part(full):
        block = own // per
        if per == 1:
            return full[block]
        value = full[block, :, :w]
        for h in range(1, per):
            value = jnp.where(
                lax.rem(own, per) == h, full[block, :, h * w : (h + 1) * w], value
            )
        return value

    contribute(
        0, lambda k: theta_full[k // per, :, (k % per) * w : (k % per + 1) * w]
    )
    h_start()
    position, moment = own_part(theta_full), own_part(mom_full)
    factor = 0.5 * leap
    for e in range(STEPS):
        moment = moment + factor * (reduced(e) - position)
        position = position + leap * moment
        factor = leap if e + 1 < STEPS else 0.5 * leap
        state[e] = position
        on_owner(r, functools.partial(spread, e))
        if e + 1 < STEPS or STEPS == 1:
            h_pass(0)
        gathered(e)
        contribute(e + 1, functools.partial(lambda k, e: state_recv[e, k], e=e))
        if e == STEPS - 1:
            finish(0)
        h_pass(1 + e)
    moment = moment + factor * (reduced(STEPS) - position)
    state[STEPS] = moment
    on_owner(r, functools.partial(spread, STEPS))
    for i in range(1 + STEPS, F):
        h_pass(i)
    gathered(STEPS)
    finish(1)
    write(0, theta_out)

    def h_add(i):
        pair = lax.rem(a + 1 + i, A)
        g_in(pair).wait_recv()
        hess_out[...] += h_recv2[pair].astype(F32)

    each(A - 1, h_add)
    write(1, mom_out)

    for c in range(PIECES):
        for i in range(F // 2):
            x_out(i, c).wait_send()
        for i in range(1, F // 2):
            x_forward(i, c).wait_send()
    for i in range(F - 1):
        for number in range(3):
            small(i, number).wait_send()
        for number in range(2):
            o_out(number, i).wait_send()
    each(R - 1, lambda i: count_out(i).wait_send())
    for e in range(STEPS + 1):
        each(
            R - 1,
            lambda i: on_owner(row_peer(i), lambda: c_out(e, i).wait_send()),
        )
        on_owner(r, lambda: each(R - 1, lambda i: p_out(e, i).wait_send()))
    each(A, lambda pair: h_out(pair).wait_send())
    each(A - 1, lambda i: g_out(lax.rem(a + 1 + i, A)).wait_send())


def shards(slab_rows, labels, center, theta_start, momentum, step_size, sample_index, sample_count):
    R, F = lax.axis_size("rows"), lax.axis_size("feat")
    rows, wide = slab_rows.shape
    whole_rows = rows * R
    full = wide * F
    chains = theta_start.shape[0]
    group = chains // F
    S = min(R, full // LANES)
    w = full // S
    cw = full // R
    A = R // 2
    live = jnp.arange(sample_index.shape[0], dtype=jnp.int32) < sample_count[0]
    slot_row = jnp.where(live, sample_index, -1)
    mult = jnp.sum(
        (slot_row[:, None] == jnp.arange(rows, dtype=jnp.int32)[None, :]).astype(F32), axis=0
    )[None, :]
    count = jnp.broadcast_to(sample_count.astype(F32)[None, :], (8, LANES))
    center_rows = jnp.broadcast_to(center[None, :], (group, wide))
    leap = (step_size * math.sqrt(full / whole_rows))[:, None]
    vmem = pl.BlockSpec(memory_space=pltpu.VMEM)
    dma = pltpu.SemaphoreType.DMA
    steps = STEPS + 1
    per = wide // w
    theta, moment, hess = pl.pallas_call(
        functools.partial(kernel, R, F, S, whole_rows),
        out_shape=(
            jax.ShapeDtypeStruct((chains, wide), F32),
            jax.ShapeDtypeStruct((chains, wide), F32),
            jax.ShapeDtypeStruct((cw, wide), F32),
        ),
        in_specs=[vmem] * 8,
        out_specs=(vmem,) * 3,
        scratch_shapes=[
            pltpu.VMEM((F, rows, wide), BF16),
            pltpu.VMEM((F, group, wide), F32),
            pltpu.VMEM((F, group, wide), F32),
            pltpu.VMEM((F, group, wide), F32),
            pltpu.VMEM((R, 8, LANES), F32),
            pltpu.VMEM((steps, S, group, w), F32),
            pltpu.VMEM((steps, R, group, w), F32),
            pltpu.VMEM((steps, group, w), F32),
            pltpu.VMEM((steps, S, group, w), F32),
            pltpu.VMEM((2, F, per, group, w), F32),
            pltpu.VMEM((full, wide), F32),
            pltpu.VMEM((full, wide), BF16),
            pltpu.VMEM((A, cw, wide), BF16),
            pltpu.VMEM((A, cw, wide), BF16),
            pltpu.VMEM((A, cw, wide), BF16),
            dma((F // 2, PIECES)),
            dma((F, PIECES)),
            dma((F // 2, PIECES)),
            dma((3, F)),
            dma((3, F)),
            dma((R,)),
            dma((R,)),
            dma((steps, R)),
            dma((steps, R)),
            dma((steps, R)),
            dma((steps, R)),
            dma((2, F)),
            dma((2, F)),
            dma((A,)),
            dma((A,)),
            dma((A,)),
            dma((A,)),
        ],
        compiler_params=pltpu.CompilerParams(
            collective_id=0, has_side_effects=True, vmem_limit_bytes=48 * 1024 * 1024
        ),
    )(
        slab_rows,
        labels.astype(F32)[None, :],
        mult,
        count,
        center_rows,
        theta_start,
        momentum,
        leap,
    )
    return theta, moment, hess.T


def solution(mesh):
    return jax.shard_map(
        shards,
        mesh=mesh,
        in_specs=(
            P("rows", "feat"),
            P("rows"),
            P("feat"),
            P(None, "feat"),
            P(None, "feat"),
            P(),
            P("rows"),
            P("rows"),
        ),
        out_specs=(P(None, "feat"), P(None, "feat"), P("feat", "rows")),
        check_vma=False,
    )
```

```python
import functools
import math

import jax
import jax.numpy as jnp
from jax import lax
from jax.experimental import pallas as pl
from jax.experimental.pallas import tpu as pltpu
from jax.sharding import PartitionSpec as P

STEPS = 2
LANES = 128
PIECES = 4
MESH = pl.DeviceIdType.MESH
F32, BF16 = jnp.float32, jnp.bfloat16


def each(count, body, limit=8):
    if count <= limit:
        for number in range(count):
            body(number)
    else:
        lax.fori_loop(0, count, lambda number, none: (body(number), none)[1], 0)


def dot(left, right, left_dim, right_dim):
    return lax.dot_general(
        left, right, (((left_dim,), (right_dim,)), ((), ())), preferred_element_type=F32
    )


def split(value):
    high = value.astype(BF16)
    return high, (value - high.astype(F32)).astype(BF16)


def kernel(
    R, F, S, whole_rows,
    x_ref, label_ref, mult_ref, count_ref, center_ref, theta_ref, mom_ref, leap_ref,
    theta_out, mom_out, hess_out,
    x_full, theta_full, mom_full, logit_part, logit_full, count_full,
    c_send, c_recv, near, near_recv, state, state_recv, final_recv,
    scaled_ref, h_part, h_send, h_recv, h_send2, h_recv2, h_recv3,
    x_ssem, x_rsem, x_fsem, s_ssem, s_rsem, n_ssem, n_rsem,
    c_ssem, c_rsem, p_ssem, p_rsem, q_ssem, q_rsem, o_ssem, o_rsem,
    h_ssem, h_rsem, g_ssem, g_rsem, k_ssem, k_rsem,
):
    rows, wide = x_ref.shape
    group = theta_ref.shape[0] // F
    w = c_send.shape[-1]
    per = wide // w
    A = R // 2
    cw = hess_out.shape[0]
    r, f = lax.axis_index("rows"), lax.axis_index("feat")
    a, b = r // 2, lax.rem(r, 2)
    mate = f + 1 - 2 * lax.rem(f, 2)
    piece = rows // PIECES

    def copy(src, dst, ssem, rsem, row, feat):
        return pltpu.make_async_remote_copy(
            src_ref=src, dst_ref=dst, send_sem=ssem, recv_sem=rsem,
            device_id=(row, feat), device_id_type=MESH,
        )

    def row_peer(i):
        return lax.rem(r + i + 1, R)

    barrier = pltpu.get_barrier_semaphore()
    at_once = jnp.broadcast_to(center_ref[...], (8, wide))
    high, low = split(at_once)
    both = jnp.concatenate([high.astype(F32), low.astype(F32)], 0).astype(BF16)

    def greet_row(i):
        pl.semaphore_signal(barrier, inc=1, device_id=(row_peer(i), f), device_id_type=MESH)

    def greet_feat(i):
        pl.semaphore_signal(
            barrier, inc=1, device_id=(r, lax.rem(f + i + 1, F)), device_id_type=MESH
        )

    each(R - 1, greet_row)
    each(F - 1, greet_feat)
    logit_part[...] = dot(both, x_ref[...], 1, 1)
    pl.semaphore_wait(barrier, R + F - 2)

    def small(i, number):
        peer = lax.rem(f + i + 1, F)
        theirs = pl.ds(pl.multiple_of(peer * group, group), group)
        src = (logit_part, theta_ref.at[theirs], mom_ref.at[theirs])[number]
        dst = (logit_full, theta_full, mom_full)[number].at[f]
        return copy(src, dst, s_ssem.at[number, peer], s_rsem.at[number, f], r, peer)

    def small_in(i, number):
        peer = lax.rem(f + i + 1, F)
        dst = (logit_full, theta_full, mom_full)[number].at[peer]
        return copy(dst, dst, s_ssem.at[number, peer], s_rsem.at[number, peer], r, peer)

    def part(c):
        return pl.ds(c * piece, piece)

    def x_out(i, c):
        peer = mate if i == 0 else lax.rem(f + 2 * i, F)
        return copy(
            x_ref.at[part(c)], x_full.at[f, part(c)], x_ssem.at[i, c], x_rsem.at[f, c], r, peer
        )

    def x_in(block, c):
        dst = x_full.at[block, part(c)]
        return copy(dst, dst, x_ssem.at[0, c], x_rsem.at[block, c], r, mate)

    def x_forward(i, c):
        block = lax.rem(f + 2 * i, F)
        dst = x_full.at[block, part(c)]
        return copy(dst, dst, x_fsem.at[i, c], x_rsem.at[block, c], r, mate)

    def count_out(i):
        peer = row_peer(i)
        return copy(count_ref, count_full.at[r], n_ssem.at[peer], n_rsem.at[r], peer, f)

    def count_in(i):
        peer = row_peer(i)
        dst = count_full.at[peer]
        return copy(dst, dst, n_ssem.at[peer], n_rsem.at[peer], peer, f)

    for i in range(F - 1):
        small(i, 0).start()
    for c in range(PIECES):
        for i in range(1, F // 2):
            x_out(i, c).start()
        if c == 0:
            for i in range(F - 1):
                for number in range(1, 3):
                    small(i, number).start()
            each(R - 1, lambda i: count_out(i).start())
    for c in range(PIECES):
        x_out(0, c).start()

    mine = pl.ds(pl.multiple_of(f * group, group), group)
    logit_full[f] = logit_part[...]
    theta_full[f] = theta_ref[mine]
    mom_full[f] = mom_ref[mine]
    x_full[f] = x_ref[...]
    count_full[r] = count_ref[...]
    leap = leap_ref[mine, :]

    for i in range(F - 1):
        small_in(i, 0).wait_recv()

    at_center = jnp.zeros((16, rows), F32)
    for g in range(F):
        at_center += logit_full[g]
    logit_hat = at_center[:1]
    center_all = at_center[:1] + at_center[8:9]
    prob_hat = jax.nn.sigmoid(logit_hat)
    weight = prob_hat * (1.0 - prob_hat)
    residual = (label_ref[...].astype(F32) - prob_hat).astype(BF16).astype(F32)

    def c_out(e, i):
        peer = row_peer(i)
        return copy(
            c_send.at[e, lax.rem(peer, S)], c_recv.at[e, r], c_ssem.at[e, peer],
            c_rsem.at[e, r], peer, f,
        )

    def c_in(e, i):
        peer = row_peer(i)
        dst = c_recv.at[e, peer]
        return copy(dst, dst, c_ssem.at[e, peer], c_rsem.at[e, peer], peer, f)

    def on_owner(number, body):
        if S == R:
            body()
        else:
            pl.when(number < S)(body)

    def contribute(e, chunk_of):
        now = jnp.zeros((2 * group if e == 0 else group, rows), F32)
        for k in range(S):
            columns = x_full[k // per, :, (k % per) * w : (k % per + 1) * w]
            if e == 0:
                now += dot(jnp.concatenate(split(chunk_of(k)), 0), columns, 1, 1)
            else:
                now += dot(chunk_of(k), columns, 1, 1)
        logit_now = now[:group]
        offset = (now[:group] + now[group:] if e == 0 else now) - center_all
        remainder = prob_hat - jax.nn.sigmoid(logit_now) + weight * (logit_now - logit_hat)
        remainder = remainder.astype(BF16).astype(F32)
        coef = residual - weight * offset + mult_ratio * remainder
        high, low = split(coef)
        both = jnp.concatenate([high, low], 0)
        for g in range(F):
            value = dot(both, x_full[g], 1, 0)
            value = value[:group] + value[group:]
            for h in range(per):
                c_send[e, g * per + h] = value[:, h * w : (h + 1) * w].astype(BF16)

        def send(i):
            on_owner(row_peer(i), lambda: c_out(e, i).start())

        each(R - 1, send)

    def reduced(e):
        on_owner(r, lambda: each(R - 1, lambda i: c_in(e, i).wait_recv()))
        c_recv[e, r] = c_send[e, lax.rem(r, S)]
        return lax.fori_loop(0, R, lambda i, acc: acc + c_recv[e, i].astype(F32), jnp.zeros((group, w), F32))

    own = lax.rem(r, S)
    rounded = near, near_recv, p_ssem, p_rsem
    whole = state, state_recv, q_ssem, q_rsem

    def p_out(kind, e, i):
        peer = row_peer(i)
        source, target, ssem, rsem = kind
        return copy(source.at[e], target.at[e, own], ssem.at[e, peer], rsem.at[e, own], peer, f)

    def p_in(kind, e, i):
        peer = lax.rem(row_peer(i), S)
        _, target, ssem, rsem = kind
        dst = target.at[e, peer]
        return copy(dst, dst, ssem.at[e, peer], rsem.at[e, peer], row_peer(i), f)

    def spread(kind, e):
        each(R - 1, lambda i: p_out(kind, e, i).start())
        kind[1][e, own] = kind[0][e]

    def gathered(kind, e):
        def take(i):
            on_owner(row_peer(i), lambda: p_in(kind, e, i).wait_recv())

        each(R - 1, take)

    def h_out(pair):
        rows_there = pl.ds(pl.multiple_of((2 * pair + 1 - b) * cw, cw), cw)
        return copy(
            h_send.at[rows_there], h_recv.at[pair], h_ssem.at[pair], h_rsem.at[pair],
            2 * a + 1 - b, f,
        )

    def g_out(pair):
        return copy(
            h_send2.at[pair], h_recv2.at[pair], g_ssem.at[pair], g_rsem.at[pair],
            2 * (a + 1 - 2 * lax.rem(a, 2)) + b, f,
        )

    def k_out(pair):
        return copy(
            h_send2.at[pair], h_recv3.at[a], k_ssem.at[pair], k_rsem.at[a], 2 * pair + b, f
        )

    def k_in(pair):
        dst = h_recv3.at[pair]
        return copy(dst, dst, k_ssem.at[pair], k_rsem.at[pair], 2 * pair + b, f)

    def own_rows(pair):
        return pl.ds(pl.multiple_of((2 * pair + b) * cw, cw), cw)

    def alike(j):
        return lax.rem(a + 2 * j, A)

    many = A // F

    def block_at(i):
        return lax.rem((f if i % 2 == 0 else mate) + 2 * (i // 2), F)

    column = jnp.transpose(jnp.broadcast_to(weight, (LANES, rows)))[:, :1]
    scaled_ref[...] = (column * x_ref[...].astype(F32)).astype(BF16)

    def h_block(i):
        g = block_at(i)
        value = dot(x_full[g], scaled_ref[...], 0, 0)
        where = pl.ds(pl.multiple_of(g * wide, wide), wide)
        h_part[where, :] = value
        h_send[where, :] = value.astype(BF16)
        each(many, lambda j: h_out(g * many + j).start())

    def h_pass(i):
        def one(j):
            pair = block_at(i) * many + j
            h_out(pair).wait_recv()
            value = h_part[own_rows(pair), :] + h_recv[pair].astype(F32)

            @pl.when(lax.rem(pair, 2) == lax.rem(a, 2))
            def _():
                h_part[own_rows(pair), :] = value

            @pl.when(lax.rem(pair, 2) != lax.rem(a, 2))
            def _():
                h_send2[pair] = value.astype(BF16)
                g_out(pair).start()

        each(many, one)

    def h_across(j):
        pair = alike(j + 1)
        g_out(pair).wait_recv()
        value = h_part[own_rows(pair), :] + h_recv2[pair].astype(F32)
        h_send2[pair] = value.astype(BF16)
        k_out(pair).start()

    def o_out(number, i):
        peer = lax.rem(f + i + 1, F)
        theirs = pl.ds(peer * per, per)
        return copy(
            state_recv.at[number, theirs], final_recv.at[number, f], o_ssem.at[number, peer],
            o_rsem.at[number, f], r, peer,
        )

    def o_in(number, i):
        peer = lax.rem(f + i + 1, F)
        dst = final_recv.at[number, peer]
        return copy(dst, dst, o_ssem.at[number, peer], o_rsem.at[number, peer], r, peer)

    def finish(number):
        for i in range(F - 1):
            o_out(number, i).start()
        for h in range(per):
            final_recv[number, f, h] = state_recv[number, f * per + h]

    def write(number, out):
        for i in range(F - 1):
            o_in(number, i).wait_recv()
        for g in range(F):
            for h in range(per):
                out[g * group : (g + 1) * group, h * w : (h + 1) * w] = final_recv[number, g, h]

    def own_part(full):
        block = own // per
        if per == 1:
            return full[block]
        value = full[block, :, :w]
        for h in range(1, per):
            value = jnp.where(
                lax.rem(own, per) == h, full[block, :, h * w : (h + 1) * w], value
            )
        return value

    h_block(0)
    for c in range(PIECES):
        x_in(mate, c).wait_recv()
    h_block(1)
    for c in range(PIECES):
        for i in range(1, F // 2):
            x_in(lax.rem(f + 2 * i, F), c).wait_recv()
            x_forward(i, c).start()
    for i in range(F - 1):
        for number in range(1, 3):
            small_in(i, number).wait_recv()
    each(R - 1, lambda i: count_in(i).wait_recv())
    total = lax.fori_loop(0, R, lambda i, acc: acc + count_full[i], jnp.zeros_like(count_ref))
    mult_ratio = mult_ref[...] * (float(whole_rows) / total[:1, :1])
    for c in range(PIECES):
        for i in range(1, F // 2):
            x_in(lax.rem(mate + 2 * i, F), c).wait_recv()

    contribute(
        0, lambda k: theta_full[k // per, :, (k % per) * w : (k % per + 1) * w]
    )
    for i in range(2, F):
        h_block(i)
    position, moment = own_part(theta_full), own_part(mom_full)
    factor = 0.5 * leap
    for e in range(STEPS):
        moment = moment + factor * (reduced(e) - position)
        position = position + leap * moment
        factor = leap if e + 1 < STEPS else 0.5 * leap
        near[e] = position.astype(BF16)
        on_owner(r, functools.partial(spread, rounded, e))
        if e == STEPS - 1:
            state[0] = position
            on_owner(r, functools.partial(spread, whole, 0))
        gathered(rounded, e)
        contribute(e + 1, functools.partial(lambda k, e: near_recv[e, k], e=e))
        if e == STEPS - 1:
            gathered(whole, 0)
            finish(0)
        if e == 1:
            for i in range(F):
                h_pass(i)
    moment = moment + factor * (reduced(STEPS) - position)
    state[1] = moment
    on_owner(r, functools.partial(spread, whole, 1))
    each(A // 2 - 1, h_across)
    gathered(whole, 1)
    finish(1)
    write(0, theta_out)

    g_out(a).wait_recv()
    hess_out[...] = h_part[own_rows(a), :] + h_recv2[a].astype(F32)

    def h_add(j):
        pair = alike(j + 1)
        k_in(pair).wait_recv()
        hess_out[...] += h_recv3[pair].astype(F32)

    each(A // 2 - 1, h_add)
    write(1, mom_out)

    for c in range(PIECES):
        for i in range(F // 2):
            x_out(i, c).wait_send()
        for i in range(1, F // 2):
            x_forward(i, c).wait_send()
    for i in range(F - 1):
        for number in range(3):
            small(i, number).wait_send()
        for number in range(2):
            o_out(number, i).wait_send()
    each(R - 1, lambda i: count_out(i).wait_send())
    for e in range(STEPS + 1):
        each(
            R - 1,
            lambda i: on_owner(row_peer(i), lambda: c_out(e, i).wait_send()),
        )
    for e in range(STEPS):
        on_owner(r, lambda: each(R - 1, lambda i: p_out(rounded, e, i).wait_send()))
    for e in range(2):
        on_owner(r, lambda: each(R - 1, lambda i: p_out(whole, e, i).wait_send()))
    each(A, lambda pair: h_out(pair).wait_send())
    each(A // 2, lambda j: g_out(lax.rem(a + 1 + 2 * j, A)).wait_send())
    each(A // 2 - 1, lambda j: k_out(alike(j + 1)).wait_send())


def shards(slab_rows, labels, center, theta_start, momentum, step_size, sample_index, sample_count):
    R, F = lax.axis_size("rows"), lax.axis_size("feat")
    rows, wide = slab_rows.shape
    whole_rows = rows * R
    full = wide * F
    chains = theta_start.shape[0]
    group = chains // F
    S = min(R, full // LANES)
    w = full // S
    cw = full // R
    A = R // 2
    live = jnp.arange(sample_index.shape[0], dtype=jnp.int32) < sample_count[0]
    slot_row = jnp.where(live, sample_index, -1)
    mult = jnp.sum(
        (slot_row[:, None] == jnp.arange(rows, dtype=jnp.int32)[None, :]).astype(F32), axis=0
    )[None, :]
    count = jnp.broadcast_to(sample_count.astype(F32)[None, :], (8, LANES))
    leap = (step_size * math.sqrt(full / whole_rows))[:, None]
    vmem = pl.BlockSpec(memory_space=pltpu.VMEM)
    dma = pltpu.SemaphoreType.DMA
    steps = STEPS + 1
    per = wide // w
    theta, moment, hess = pl.pallas_call(
        functools.partial(kernel, R, F, S, whole_rows),
        out_shape=(
            jax.ShapeDtypeStruct((chains, wide), F32),
            jax.ShapeDtypeStruct((chains, wide), F32),
            jax.ShapeDtypeStruct((cw, wide), F32),
        ),
        in_specs=[vmem] * 8,
        out_specs=(vmem,) * 3,
        scratch_shapes=[
            pltpu.VMEM((F, rows, wide), BF16),
            pltpu.VMEM((F, group, wide), F32),
            pltpu.VMEM((F, group, wide), F32),
            pltpu.VMEM((16, rows), F32),
            pltpu.VMEM((F, 16, rows), F32),
            pltpu.VMEM((R, 8, LANES), F32),
            pltpu.VMEM((steps, S, group, w), BF16),
            pltpu.VMEM((steps, R, group, w), BF16),
            pltpu.VMEM((STEPS, group, w), BF16),
            pltpu.VMEM((STEPS, S, group, w), BF16),
            pltpu.VMEM((2, group, w), F32),
            pltpu.VMEM((2, S, group, w), F32),
            pltpu.VMEM((2, F, per, group, w), F32),
            pltpu.VMEM((rows, wide), BF16),
            pltpu.VMEM((full, wide), F32),
            pltpu.VMEM((full, wide), BF16),
            pltpu.VMEM((A, cw, wide), BF16),
            pltpu.VMEM((A, cw, wide), BF16),
            pltpu.VMEM((A, cw, wide), BF16),
            pltpu.VMEM((A, cw, wide), BF16),
            dma((F // 2, PIECES)),
            dma((F, PIECES)),
            dma((F // 2, PIECES)),
            dma((3, F)),
            dma((3, F)),
            dma((R,)),
            dma((R,)),
            dma((steps, R)),
            dma((steps, R)),
            dma((STEPS, R)),
            dma((STEPS, R)),
            dma((2, R)),
            dma((2, R)),
            dma((2, F)),
            dma((2, F)),
            dma((A,)),
            dma((A,)),
            dma((A,)),
            dma((A,)),
            dma((A,)),
            dma((A,)),
        ],
        compiler_params=pltpu.CompilerParams(
            collective_id=0, has_side_effects=True, vmem_limit_bytes=48 * 1024 * 1024
        ),
    )(
        slab_rows,
        labels[None, :],
        mult,
        count,
        center[None, :],
        theta_start,
        momentum,
        leap,
    )
    return theta, moment, hess.T


def solution(mesh):
    return jax.shard_map(
        shards,
        mesh=mesh,
        in_specs=(
            P("rows", "feat"),
            P("rows"),
            P("feat"),
            P(None, "feat"),
            P(None, "feat"),
            P(),
            P("rows"),
            P("rows"),
        ),
        out_specs=(P(None, "feat"), P(None, "feat"), P("feat", "rows")),
        check_vma=False,
    )
```

```python
import functools
import math

import jax
import jax.numpy as jnp
from jax import lax
from jax.experimental import pallas as pl
from jax.experimental.pallas import tpu as pltpu
from jax.sharding import PartitionSpec as P

STEPS = 2
LANES = 128
PIECES = 4
MESH = pl.DeviceIdType.MESH
F32, BF16 = jnp.float32, jnp.bfloat16


def each(count, body, limit=8):
    if count <= limit:
        for number in range(count):
            body(number)
    else:
        lax.fori_loop(0, count, lambda number, none: (body(number), none)[1], 0)


def dot(left, right, left_dim, right_dim):
    return lax.dot_general(
        left, right, (((left_dim,), (right_dim,)), ((), ())), preferred_element_type=F32
    )


def split(value):
    high = value.astype(BF16)
    return high, (value - high.astype(F32)).astype(BF16)


def kernel(
    R, F, S, whole_rows,
    x_ref, label_ref, mult_ref, count_ref, center_ref, theta_ref, mom_ref, leap_ref,
    theta_out, mom_out, hess_out,
    x_full, theta_full, mom_full, logit_part, logit_full, count_full,
    c_send, c_recv, near, near_recv, state, state_recv, final_recv,
    scaled_ref, h_part, h_send, h_recv, h_send2, h_recv2, h_recv3,
    x_ssem, x_rsem, x_fsem, s_ssem, s_rsem, n_ssem, n_rsem,
    c_ssem, c_rsem, p_ssem, p_rsem, q_ssem, q_rsem, o_ssem, o_rsem,
    h_ssem, h_rsem, g_ssem, g_rsem, k_ssem, k_rsem,
):
    rows, wide = x_ref.shape
    group = theta_ref.shape[0] // F
    w = c_send.shape[-1]
    per = wide // w
    A = R // 2
    cw = hess_out.shape[0]
    r, f = lax.axis_index("rows"), lax.axis_index("feat")
    a, b = r // 2, lax.rem(r, 2)
    mate = f + 1 - 2 * lax.rem(f, 2)
    piece = rows // PIECES

    def copy(src, dst, ssem, rsem, row, feat):
        return pltpu.make_async_remote_copy(
            src_ref=src, dst_ref=dst, send_sem=ssem, recv_sem=rsem,
            device_id=(row, feat), device_id_type=MESH,
        )

    def row_peer(i):
        return lax.rem(r + i + 1, R)

    barrier = pltpu.get_barrier_semaphore()
    at_once = jnp.broadcast_to(center_ref[...], (8, wide))
    high, low = split(at_once)
    both = jnp.concatenate([high.astype(F32), low.astype(F32)], 0).astype(BF16)

    def greet_row(i):
        pl.semaphore_signal(barrier, inc=1, device_id=(row_peer(i), f), device_id_type=MESH)

    def greet_feat(i):
        pl.semaphore_signal(
            barrier, inc=1, device_id=(r, lax.rem(f + i + 1, F)), device_id_type=MESH
        )

    each(R - 1, greet_row)
    each(F - 1, greet_feat)
    logit_part[...] = dot(both, x_ref[...], 1, 1)
    pl.semaphore_wait(barrier, R + F - 2)

    def small(i, number):
        peer = lax.rem(f + i + 1, F)
        theirs = pl.ds(pl.multiple_of(peer * group, group), group)
        src = (logit_part, theta_ref.at[theirs], mom_ref.at[theirs])[number]
        dst = (logit_full, theta_full, mom_full)[number].at[f]
        return copy(src, dst, s_ssem.at[number, peer], s_rsem.at[number, f], r, peer)

    def small_in(i, number):
        peer = lax.rem(f + i + 1, F)
        dst = (logit_full, theta_full, mom_full)[number].at[peer]
        return copy(dst, dst, s_ssem.at[number, peer], s_rsem.at[number, peer], r, peer)

    def part(c):
        return pl.ds(c * piece, piece)

    def x_out(i, c):
        peer = mate if i == 0 else lax.rem(f + 2 * i, F)
        return copy(
            x_ref.at[part(c)], x_full.at[f, part(c)], x_ssem.at[i, c], x_rsem.at[f, c], r, peer
        )

    def x_in(block, c):
        dst = x_full.at[block, part(c)]
        return copy(dst, dst, x_ssem.at[0, c], x_rsem.at[block, c], r, mate)

    def x_forward(i, c):
        block = lax.rem(f + 2 * i, F)
        dst = x_full.at[block, part(c)]
        return copy(dst, dst, x_fsem.at[i, c], x_rsem.at[block, c], r, mate)

    def count_out(i):
        peer = row_peer(i)
        return copy(count_ref, count_full.at[r], n_ssem.at[peer], n_rsem.at[r], peer, f)

    def count_in(i):
        peer = row_peer(i)
        dst = count_full.at[peer]
        return copy(dst, dst, n_ssem.at[peer], n_rsem.at[peer], peer, f)

    for i in range(F - 1):
        small(i, 0).start()
    for c in range(PIECES):
        for i in range(1, F // 2):
            x_out(i, c).start()
        if c == 0:
            for i in range(F - 1):
                for number in range(1, 3):
                    small(i, number).start()
            each(R - 1, lambda i: count_out(i).start())
    for c in range(PIECES):
        x_out(0, c).start()

    mine = pl.ds(pl.multiple_of(f * group, group), group)
    logit_full[f] = logit_part[...]
    theta_full[f] = theta_ref[mine]
    mom_full[f] = mom_ref[mine]
    x_full[f] = x_ref[...]
    count_full[r] = count_ref[...]
    leap = leap_ref[mine, :]

    for i in range(F - 1):
        small_in(i, 0).wait_recv()

    at_center = jnp.zeros((16, rows), F32)
    for g in range(F):
        at_center += logit_full[g]
    logit_hat = at_center[:1]
    center_all = at_center[:1] + at_center[8:9]
    prob_hat = jax.nn.sigmoid(logit_hat)
    weight = prob_hat * (1.0 - prob_hat)
    residual = (label_ref[...].astype(F32) - prob_hat).astype(BF16).astype(F32)

    def c_out(e, i):
        peer = row_peer(i)
        return copy(
            c_send.at[e, lax.rem(peer, S)], c_recv.at[e, r], c_ssem.at[e, peer],
            c_rsem.at[e, r], peer, f,
        )

    def c_in(e, i):
        peer = row_peer(i)
        dst = c_recv.at[e, peer]
        return copy(dst, dst, c_ssem.at[e, peer], c_rsem.at[e, peer], peer, f)

    def on_owner(number, body):
        if S == R:
            body()
        else:
            pl.when(number < S)(body)

    def contribute(e, chunk_of):
        now = jnp.zeros((2 * group if e == 0 else group, rows), F32)
        for k in range(S):
            columns = x_full[k // per, :, (k % per) * w : (k % per + 1) * w]
            if e == 0:
                now += dot(jnp.concatenate(split(chunk_of(k)), 0), columns, 1, 1)
            else:
                now += dot(chunk_of(k), columns, 1, 1)
        logit_now = now[:group]
        offset = (now[:group] + now[group:] if e == 0 else now) - center_all
        remainder = prob_hat - jax.nn.sigmoid(logit_now) + weight * (logit_now - logit_hat)
        remainder = remainder.astype(BF16).astype(F32)
        coef = residual - weight * offset + mult_ratio * remainder
        high, low = split(coef)
        both = jnp.concatenate([high, low], 0)
        for g in range(F):
            value = dot(both, x_full[g], 1, 0)
            value = value[:group] + value[group:]
            for h in range(per):
                c_send[e, g * per + h] = value[:, h * w : (h + 1) * w].astype(BF16)

        def send(i):
            on_owner(row_peer(i), lambda: c_out(e, i).start())

        each(R - 1, send)

    def reduced(e):
        on_owner(r, lambda: each(R - 1, lambda i: c_in(e, i).wait_recv()))
        c_recv[e, r] = c_send[e, lax.rem(r, S)]
        return lax.fori_loop(0, R, lambda i, acc: acc + c_recv[e, i].astype(F32), jnp.zeros((group, w), F32))

    own = lax.rem(r, S)
    rounded = near, near_recv, p_ssem, p_rsem
    whole = state, state_recv, q_ssem, q_rsem

    def p_out(kind, e, i):
        peer = row_peer(i)
        source, target, ssem, rsem = kind
        return copy(source.at[e], target.at[e, own], ssem.at[e, peer], rsem.at[e, own], peer, f)

    def p_in(kind, e, i):
        peer = lax.rem(row_peer(i), S)
        _, target, ssem, rsem = kind
        dst = target.at[e, peer]
        return copy(dst, dst, ssem.at[e, peer], rsem.at[e, peer], row_peer(i), f)

    def spread(kind, e):
        each(R - 1, lambda i: p_out(kind, e, i).start())
        kind[1][e, own] = kind[0][e]

    def gathered(kind, e):
        def take(i):
            on_owner(row_peer(i), lambda: p_in(kind, e, i).wait_recv())

        each(R - 1, take)

    def h_out(pair):
        rows_there = pl.ds(pl.multiple_of((2 * pair + 1 - b) * cw, cw), cw)
        return copy(
            h_send.at[rows_there], h_recv.at[pair], h_ssem.at[pair], h_rsem.at[pair],
            2 * a + 1 - b, f,
        )

    def g_out(pair):
        return copy(
            h_send2.at[pair], h_recv2.at[pair], g_ssem.at[pair], g_rsem.at[pair],
            2 * (a + 1 - 2 * lax.rem(a, 2)) + b, f,
        )

    def k_out(pair):
        return copy(
            h_send2.at[pair], h_recv3.at[a], k_ssem.at[pair], k_rsem.at[a], 2 * pair + b, f
        )

    def k_in(pair):
        dst = h_recv3.at[pair]
        return copy(dst, dst, k_ssem.at[pair], k_rsem.at[pair], 2 * pair + b, f)

    def own_rows(pair):
        return pl.ds(pl.multiple_of((2 * pair + b) * cw, cw), cw)

    def alike(j):
        return lax.rem(a + 2 * j, A)

    many = A // F

    def block_at(i):
        return lax.rem((f if i % 2 == 0 else mate) + 2 * (i // 2), F)

    column = jnp.transpose(jnp.broadcast_to(weight, (LANES, rows)))[:, :1]
    scaled_ref[...] = (column * x_ref[...].astype(F32)).astype(BF16)

    def h_block(i):
        g = block_at(i)
        value = dot(x_full[g], scaled_ref[...], 0, 0)
        where = pl.ds(pl.multiple_of(g * wide, wide), wide)
        h_part[where, :] = value
        h_send[where, :] = value.astype(BF16)
        each(many, lambda j: h_out(g * many + j).start())

    def h_pass(i):
        def one(j):
            pair = block_at(i) * many + j
            h_out(pair).wait_recv()
            value = h_part[own_rows(pair), :] + h_recv[pair].astype(F32)

            @pl.when(lax.rem(pair, 2) == lax.rem(a, 2))
            def _():
                h_part[own_rows(pair), :] = value

            @pl.when(lax.rem(pair, 2) != lax.rem(a, 2))
            def _():
                h_send2[pair] = value.astype(BF16)
                g_out(pair).start()

        each(many, one)

    def h_across(j):
        pair = alike(j + 1)
        g_out(pair).wait_recv()
        value = h_part[own_rows(pair), :] + h_recv2[pair].astype(F32)
        h_send2[pair] = value.astype(BF16)
        k_out(pair).start()

    def o_out(number, i):
        peer = lax.rem(f + i + 1, F)
        theirs = pl.ds(peer * per, per)
        return copy(
            state_recv.at[number, theirs], final_recv.at[number, f], o_ssem.at[number, peer],
            o_rsem.at[number, f], r, peer,
        )

    def o_in(number, i):
        peer = lax.rem(f + i + 1, F)
        dst = final_recv.at[number, peer]
        return copy(dst, dst, o_ssem.at[number, peer], o_rsem.at[number, peer], r, peer)

    def finish(number):
        for i in range(F - 1):
            o_out(number, i).start()
        for h in range(per):
            final_recv[number, f, h] = state_recv[number, f * per + h]

    def write(number, out):
        for i in range(F - 1):
            o_in(number, i).wait_recv()
        for g in range(F):
            for h in range(per):
                out[g * group : (g + 1) * group, h * w : (h + 1) * w] = final_recv[number, g, h]

    def own_part(full):
        block = own // per
        if per == 1:
            return full[block]
        value = full[block, :, :w]
        for h in range(1, per):
            value = jnp.where(
                lax.rem(own, per) == h, full[block, :, h * w : (h + 1) * w], value
            )
        return value

    h_block(0)
    for c in range(PIECES):
        x_in(mate, c).wait_recv()
    h_block(1)
    for c in range(PIECES):
        for i in range(1, F // 2):
            x_in(lax.rem(f + 2 * i, F), c).wait_recv()
            x_forward(i, c).start()
    for i in range(F - 1):
        for number in range(1, 3):
            small_in(i, number).wait_recv()
    each(R - 1, lambda i: count_in(i).wait_recv())
    total = lax.fori_loop(0, R, lambda i, acc: acc + count_full[i], jnp.zeros_like(count_ref))
    mult_ratio = mult_ref[...] * (float(whole_rows) / total[:1, :1])
    for c in range(PIECES):
        for i in range(1, F // 2):
            x_in(lax.rem(mate + 2 * i, F), c).wait_recv()

    contribute(
        0, lambda k: theta_full[k // per, :, (k % per) * w : (k % per + 1) * w]
    )
    for i in range(2, F):
        h_block(i)
    position, moment = own_part(theta_full), own_part(mom_full)
    factor = 0.5 * leap
    for e in range(STEPS):
        moment = moment + factor * (reduced(e) - position)
        position = position + leap * moment
        factor = leap if e + 1 < STEPS else 0.5 * leap
        near[e] = position.astype(BF16)
        on_owner(r, functools.partial(spread, rounded, e))
        if e == STEPS - 1:
            state[0] = position
            on_owner(r, functools.partial(spread, whole, 0))
        if e == 1:
            for i in range(F // 2):
                h_pass(i)
        gathered(rounded, e)
        contribute(e + 1, functools.partial(lambda k, e: near_recv[e, k], e=e))
        if e == STEPS - 1:
            gathered(whole, 0)
            finish(0)
        if e == 1:
            for i in range(F // 2, F):
                h_pass(i)
    moment = moment + factor * (reduced(STEPS) - position)
    state[1] = moment
    on_owner(r, functools.partial(spread, whole, 1))
    each(A // 2 - 1, h_across)
    gathered(whole, 1)
    finish(1)
    write(0, theta_out)

    g_out(a).wait_recv()
    hess_out[...] = h_part[own_rows(a), :] + h_recv2[a].astype(F32)

    def h_add(j):
        pair = alike(j + 1)
        k_in(pair).wait_recv()
        hess_out[...] += h_recv3[pair].astype(F32)

    each(A // 2 - 1, h_add)
    write(1, mom_out)

    for c in range(PIECES):
        for i in range(F // 2):
            x_out(i, c).wait_send()
        for i in range(1, F // 2):
            x_forward(i, c).wait_send()
    for i in range(F - 1):
        for number in range(3):
            small(i, number).wait_send()
        for number in range(2):
            o_out(number, i).wait_send()
    each(R - 1, lambda i: count_out(i).wait_send())
    for e in range(STEPS + 1):
        each(
            R - 1,
            lambda i: on_owner(row_peer(i), lambda: c_out(e, i).wait_send()),
        )
    for e in range(STEPS):
        on_owner(r, lambda: each(R - 1, lambda i: p_out(rounded, e, i).wait_send()))
    for e in range(2):
        on_owner(r, lambda: each(R - 1, lambda i: p_out(whole, e, i).wait_send()))
    each(A, lambda pair: h_out(pair).wait_send())
    each(A // 2, lambda j: g_out(lax.rem(a + 1 + 2 * j, A)).wait_send())
    each(A // 2 - 1, lambda j: k_out(alike(j + 1)).wait_send())


def shards(slab_rows, labels, center, theta_start, momentum, step_size, sample_index, sample_count):
    R, F = lax.axis_size("rows"), lax.axis_size("feat")
    rows, wide = slab_rows.shape
    whole_rows = rows * R
    full = wide * F
    chains = theta_start.shape[0]
    group = chains // F
    S = min(R, full // LANES)
    w = full // S
    cw = full // R
    A = R // 2
    live = jnp.arange(sample_index.shape[0], dtype=jnp.int32) < sample_count[0]
    slot_row = jnp.where(live, sample_index, -1)
    mult = jnp.sum(
        (slot_row[:, None] == jnp.arange(rows, dtype=jnp.int32)[None, :]).astype(F32), axis=0
    )[None, :]
    count = jnp.broadcast_to(sample_count.astype(F32)[None, :], (8, LANES))
    leap = (step_size * math.sqrt(full / whole_rows))[:, None]
    vmem = pl.BlockSpec(memory_space=pltpu.VMEM)
    dma = pltpu.SemaphoreType.DMA
    steps = STEPS + 1
    per = wide // w
    theta, moment, hess = pl.pallas_call(
        functools.partial(kernel, R, F, S, whole_rows),
        out_shape=(
            jax.ShapeDtypeStruct((chains, wide), F32),
            jax.ShapeDtypeStruct((chains, wide), F32),
            jax.ShapeDtypeStruct((cw, wide), F32),
        ),
        in_specs=[vmem] * 8,
        out_specs=(vmem,) * 3,
        scratch_shapes=[
            pltpu.VMEM((F, rows, wide), BF16),
            pltpu.VMEM((F, group, wide), F32),
            pltpu.VMEM((F, group, wide), F32),
            pltpu.VMEM((16, rows), F32),
            pltpu.VMEM((F, 16, rows), F32),
            pltpu.VMEM((R, 8, LANES), F32),
            pltpu.VMEM((steps, S, group, w), BF16),
            pltpu.VMEM((steps, R, group, w), BF16),
            pltpu.VMEM((STEPS, group, w), BF16),
            pltpu.VMEM((STEPS, S, group, w), BF16),
            pltpu.VMEM((2, group, w), F32),
            pltpu.VMEM((2, S, group, w), F32),
            pltpu.VMEM((2, F, per, group, w), F32),
            pltpu.VMEM((rows, wide), BF16),
            pltpu.VMEM((full, wide), F32),
            pltpu.VMEM((full, wide), BF16),
            pltpu.VMEM((A, cw, wide), BF16),
            pltpu.VMEM((A, cw, wide), BF16),
            pltpu.VMEM((A, cw, wide), BF16),
            pltpu.VMEM((A, cw, wide), BF16),
            dma((F // 2, PIECES)),
            dma((F, PIECES)),
            dma((F // 2, PIECES)),
            dma((3, F)),
            dma((3, F)),
            dma((R,)),
            dma((R,)),
            dma((steps, R)),
            dma((steps, R)),
            dma((STEPS, R)),
            dma((STEPS, R)),
            dma((2, R)),
            dma((2, R)),
            dma((2, F)),
            dma((2, F)),
            dma((A,)),
            dma((A,)),
            dma((A,)),
            dma((A,)),
            dma((A,)),
            dma((A,)),
        ],
        compiler_params=pltpu.CompilerParams(
            collective_id=0, has_side_effects=True, vmem_limit_bytes=48 * 1024 * 1024
        ),
    )(
        slab_rows,
        labels[None, :],
        mult,
        count,
        center[None, :],
        theta_start,
        momentum,
        leap,
    )
    return theta, moment, hess.T


def solution(mesh):
    return jax.shard_map(
        shards,
        mesh=mesh,
        in_specs=(
            P("rows", "feat"),
            P("rows"),
            P("feat"),
            P(None, "feat"),
            P(None, "feat"),
            P(),
            P("rows"),
            P("rows"),
        ),
        out_specs=(P(None, "feat"), P(None, "feat"), P("feat", "rows")),
        check_vma=False,
    )
```
